32 devices in a mesh: chan: 16 (over z, y, core), stn: 2 (over x).
Axes of the slice: x: 2, y: 2, z: 4, core: 2. Of those that a mesh axis runs over, the one named last changes fastest.
Arguments:
- voltages: bfloat16 [1024, 196608], P('stn', 'chan'), may hold values from -6 to 6
- pfb_taps: float32 [16, 512], replicated, may hold values from -1.5 to 1.5
- flags: int32 [512, 256, 48], P('stn', 'chan'), may hold values 0 or 1
Outputs:
- visibilities: float32 [256, 2, 1024, 1024], P('chan', None, 'stn')
The draws below stay inside these ranges and needn't reach their ends.
All inputs are finite; a program needn't handle non-finite values. No bound on the sum of `flags` on one device may be relied on, other than what follows from the above.
Results may differ from the reference program's by a relative error of at most 0.0062.
Values may be sent and summed in bfloat16 or wider, within the bound.
No kernel may reach another device: no remote copies, remote signals or barrier semaphores. Data moves between devices by JAX's collectives and lax.ppermute only.
A program may use at most 320 MiB of HBM per device.

```python
import math
import jax
import jax.numpy as jnp
from jax import lax

STATIONS = 512
POLS = 2
CHANNELS = 256
TAPS = 16
FBLK = 8
SIGNALS = 1024
NFFT = 512
SPECTRA = 384
FBLOCKS = 48


def plant(result, stream_key, smallest, top_value):
    spot = [jax.random.randint(jax.random.fold_in(stream_key, axis), (), 0, length) for axis, length in enumerate(result.shape)]
    widest = result.shape.index(max(result.shape))
    next_to = spot[:widest] + [(spot[widest] + 1) % result.shape[widest]] + spot[widest + 1:]
    return result.at[tuple(spot)].set(smallest).at[tuple(next_to)].set(top_value)


def level_of(rng, dims, cuts, smallest, top_value):
    loudness = 1.0
    for axis_at, blocks in cuts:
        heights = jax.random.uniform(jax.random.fold_in(jax.random.fold_in(rng, 6), axis_at), (blocks,), jnp.float32, smallest / len(cuts), top_value / len(cuts))
        loudness = loudness * jnp.repeat(jnp.exp(heights), dims[axis_at] // blocks).reshape((-1,) + (1,) * (len(dims) - 1 - axis_at))
    return loudness


def noise(key, dims, scale, limit, cuts=(), kind=jnp.bfloat16):
    values = jax.random.normal(key, dims, jnp.float32) * scale
    if len(cuts) > 0:
        values = level_of(key, dims, cuts, -0.22, 0.18) * values
    return jnp.clip(values, min=-limit, max=limit).astype(kind)


def setup_inputs(seed: int = 0) -> dict:
    streams_of = jax.random.split(jax.random.key(seed), 4)
    return {
        "voltages": noise(streams_of[0], (SIGNALS, SPECTRA * NFFT), 1.0, 6.0, ((0, 2), (1, 16))),
        "pfb_taps": noise(streams_of[1], (TAPS, NFFT), 0.25, 1.5, (), jnp.float32),
        "flags": plant((jax.random.randint(streams_of[2], (STATIONS, CHANNELS, FBLOCKS), 0, 4) < 3).astype(jnp.int32), jax.random.fold_in(streams_of[2], 1), 0, 1),
    }


def dft_table(length):
    rows_index = jnp.arange(length, dtype=jnp.int32)
    chan_index = rows_index // 2
    sample_index = jnp.arange(length, dtype=jnp.int32)
    phase_step = chan_index[:, None] * sample_index[None, :] % length
    angles = phase_step.astype(jnp.float32) * (2.0 * math.pi / length)
    values = jnp.where((rows_index % 2 == 0)[:, None], jnp.cos(angles), -jnp.sin(angles))
    return (values / math.sqrt(length)).astype(jnp.bfloat16)

def reference(voltages, pfb_taps, flags):
    frames = voltages.reshape(SIGNALS, SPECTRA, NFFT)
    padded = jnp.pad(frames, ((0, 0), (TAPS - 1, 0), (0, 0)))
    filtered = jnp.zeros((SIGNALS, SPECTRA, NFFT), jnp.float32)
    for tap_index in range(TAPS):
        offset = TAPS - 1 - tap_index
        filtered = filtered + pfb_taps[tap_index] * padded[:, offset:offset + SPECTRA, :].astype(jnp.float32)
    filtered = filtered.astype(jnp.bfloat16)
    table = dft_table(NFFT)
    spectra = jnp.einsum('qn,stn->qst', table.astype(jnp.float32), filtered.astype(jnp.float32)).astype(jnp.bfloat16)
    keep = jnp.transpose(flags, (1, 0, 2)).astype(jnp.bfloat16)[:, None, :, None, :, None]
    weighted = (spectra.reshape(CHANNELS, 2, STATIONS, POLS, FBLOCKS, FBLK) * keep).reshape(CHANNELS, 2, SIGNALS, SPECTRA)

    def one_channel(block):
        block = block.astype(jnp.float32)
        prods = jnp.einsum('pat,qbt->pqab', block, block)
        real_part = prods[0, 0] + prods[1, 1]
        imag_part = prods[1, 0] - prods[0, 1]
        return jnp.stack([real_part, imag_part], axis=0) / float(SPECTRA)
    return lax.map(one_channel, weighted)
```

```python
import functools
import math

import jax
import jax.numpy as jnp
import numpy as np
from jax import lax
from jax.experimental import pallas as pl
from jax.experimental.pallas import tpu as pltpu
from jax.sharding import PartitionSpec as P

POLS = 2
LANES = 128
ROWS = 16
STEP = 8
VMEM = 56 * 1024 * 1024
BF16 = jnp.bfloat16
F32 = jnp.float32


def shifted(block, axis, distance):
    devices = range(lax.axis_size(axis))
    route = [(i - distance, i) for i in devices if i - distance in devices]
    return lax.ppermute(block, axis, route)


def swapped(block, axis, mask):
    return lax.ppermute(block, axis, [(i, i ^ mask) for i in range(lax.axis_size(axis))])


def dft_table(length):
    rows_index = np.arange(length)
    phase = (rows_index // 2)[:, None] * np.arange(length)[None, :] % length
    angles = phase.astype(np.float32) * np.float32(2.0 * math.pi / length)
    values = np.where((rows_index % 2 == 0)[:, None], np.cos(angles), -np.sin(angles))
    return (values / np.float32(math.sqrt(length))).astype(np.float32)


def spectra_kernel(start, count, has_halo, *refs):
    if has_halo:
        halo_ref, refs = refs[0], refs[1:]
    volts_ref, taps_ref, table_ref = refs[:3]
    outs, (filt_ref, res_ref) = refs[3:-2], refs[-2:]
    taps, length = taps_ref.shape
    signals = volts_ref.shape[0]

    def frame(rows, j, n0):
        if j < 0:
            return halo_ref[rows, pl.ds((j + taps - 1) * length + n0, LANES)].astype(F32)
        return volts_ref[rows, pl.ds(j * length + n0, LANES)].astype(F32)

    def body(g, carry):
        rows = pl.ds(pl.multiple_of(g * ROWS, ROWS), ROWS)
        for n0 in range(0, length, LANES):
            coef = [taps_ref[k : k + 1, n0 : n0 + LANES] for k in range(taps)]
            for t0 in range(0, count, STEP):
                sums = [None] * STEP
                for j in range(start + t0 - (taps - 1), start + t0 + STEP):
                    value = frame(rows, j, n0)
                    for t in range(STEP):
                        k = start + t0 + t - j
                        if 0 <= k < taps:
                            term = coef[k] * value
                            sums[t] = term if sums[t] is None else sums[t] + term
                for t in range(STEP):
                    filt_ref[t0 + t, rows, n0 : n0 + LANES] = sums[t].astype(BF16)
        return carry

    lax.fori_loop(0, signals // ROWS, body, 0)
    for t in range(count):
        res_ref[pl.ds(t, length, stride=count), :] = lax.dot_general(
            table_ref[...], filt_ref[t], (((1,), (1,)), ((), ())), preferred_element_type=F32
        )
    rows = length * count // len(outs)
    for i, out in enumerate(outs):
        out[...] = res_ref[i * rows : (i + 1) * rows, :].astype(BF16)


def spectra(volts, halo, taps, table, start, count, pieces):
    signals = volts.shape[0]
    length = taps.shape[1]
    block = min(LANES, signals)
    width = (start + count) * length
    rows = length * count // pieces
    in_specs = [
        pl.BlockSpec((block, width), lambda s: (s, 0)),
        pl.BlockSpec(taps.shape, lambda s: (0, 0)),
        pl.BlockSpec(table.shape, lambda s: (0, 0)),
    ]
    args = (volts, taps, table)
    if halo is not None:
        in_specs.insert(0, pl.BlockSpec((block, halo.shape[1]), lambda s: (s, 0)))
        args = (halo,) + args
    return pl.pallas_call(
        functools.partial(spectra_kernel, start, count, halo is not None),
        grid=(signals // block,),
        in_specs=in_specs,
        out_specs=[pl.BlockSpec((rows, block), lambda s: (0, s))] * pieces,
        out_shape=[jax.ShapeDtypeStruct((rows, signals), BF16)] * pieces,
        scratch_shapes=[
            pltpu.VMEM((count, block, length), BF16),
            pltpu.VMEM((length * count, block), F32),
        ],
        compiler_params=pltpu.CompilerParams(vmem_limit_bytes=VMEM),
        cost_estimate=pl.CostEstimate(
            flops=2 * length * length * count * signals * 5,
            bytes_accessed=2 * signals * (width + length * count),
            transcendentals=0,
        ),
    )(*args)


def join_kernel(count, *refs):
    pieces, keep_ref, out_ref = refs[:-2], refs[-2], refs[-1]
    blocks = count // STEP
    for c in range(out_ref.shape[0]):
        parts = [[], []]
        for p, piece in enumerate(pieces):
            values = piece[c * 2 * count : (c + 1) * 2 * count, :].astype(F32)
            for r in range(2):
                for b in range(blocks):
                    at = r * count + b * STEP
                    i = p * blocks + b
                    parts[r].append(values[at : at + STEP] * keep_ref[c, i : i + 1, :])
        for r in range(2):
            out_ref[c, r] = jnp.concatenate(parts[r], axis=0).astype(BF16)


def joined(pieces, keep, count):
    chans = keep.shape[0]
    signals = keep.shape[2]
    frames = len(pieces) * count
    group = math.gcd(chans, 4)
    return pl.pallas_call(
        functools.partial(join_kernel, count),
        grid=(chans // group,),
        in_specs=[pl.BlockSpec((group * 2 * count, signals), lambda c: (c, 0))] * len(pieces)
        + [pl.BlockSpec((group,) + keep.shape[1:], lambda c: (c, 0, 0))],
        out_specs=pl.BlockSpec((group, 2, frames, signals), lambda c: (c, 0, 0, 0)),
        out_shape=jax.ShapeDtypeStruct((chans, 2, frames, signals), BF16),
        compiler_params=pltpu.CompilerParams(vmem_limit_bytes=VMEM),
        cost_estimate=pl.CostEstimate(
            flops=chans * 2 * frames * signals,
            bytes_accessed=8 * chans * frames * signals,
            transcendentals=0,
        ),
    )(*pieces, keep)


def correlate_kernel(parts, widths, scale, place_ref, *refs):
    out_ref, (lhs_re, lhs_im, rhs) = refs[-4], refs[-3:]
    groups = len(parts)
    total = sum(parts)
    for side in range(len(widths)):
        mine = refs[side * groups : (side + 1) * groups]
        for r in range(2):
            at = r * total
            for ref, rows in zip(mine, parts):
                rhs[at : at + rows, : widths[side]] = ref[0, r]
                at += rows
        if side == 0:
            turned = rhs[:, : widths[0]].T
            lhs_re[...] = turned
            lhs_im[:, :total] = turned[:, total:]
            lhs_im[:, total:] = -turned[:, :total]
            if widths[0] != out_ref.shape[3] // len(widths):
                continue
        columns = pl.ds(pl.multiple_of(place_ref[side] * LANES, LANES), widths[side])
        for r, lhs in enumerate((lhs_re, lhs_im)):
            out_ref[0, r, :, columns] = scale * jnp.dot(
                lhs[...], rhs[:, : widths[side]], preferred_element_type=F32
            )


def correlated(result, first, chans, local, others, place, shape, scale):
    operands = local + others
    parts = [array.shape[2] for array, _ in local]
    widths = [group[0][0].shape[3] for group in (local, others)]
    signals = widths[0]
    in_specs = [
        pl.BlockSpec((1, 2) + array.shape[2:], functools.partial(lambda b, c, place: (c + b, 0, 0, 0), first - begin))
        for array, begin in operands
    ]
    args = [array for array, _ in operands]
    aliases = {}
    if result is not None:
        in_specs.append(pl.BlockSpec(memory_space=pl.ANY))
        aliases = {1 + len(args): 0}
        args.append(result)
    total = sum(parts)
    return pl.pallas_call(
        functools.partial(correlate_kernel, parts, widths, scale),
        grid_spec=pltpu.PrefetchScalarGridSpec(
            num_scalar_prefetch=1,
            grid=(chans,),
            in_specs=in_specs,
            out_specs=pl.BlockSpec((1,) + shape[1:], lambda c, place: (c + first, 0, 0, 0)),
            scratch_shapes=[
                pltpu.VMEM((signals, 2 * total), BF16),
                pltpu.VMEM((signals, 2 * total), BF16),
                pltpu.VMEM((2 * total, max(widths)), BF16),
            ],
        ),
        out_shape=jax.ShapeDtypeStruct(shape, F32),
        input_output_aliases=aliases,
        compiler_params=pltpu.CompilerParams(vmem_limit_bytes=VMEM),
        cost_estimate=pl.CostEstimate(
            flops=8 * chans * total * signals * shape[3],
            bytes_accessed=4 * chans * 2 * signals * shape[3],
            transcendentals=0,
        ),
    )(place, *args)


GROUP = 4
SPLITS = 2


def shards(voltages, pfb_taps, flags):
    taps, length = pfb_taps.shape
    signals = voltages.shape[0]
    frames = voltages.shape[1] // length
    devices = lax.axis_size("chan")
    me = lax.axis_index("chan")
    stns = lax.axis_size("stn")
    chans = length // 2 // devices
    total = frames * devices
    blocks = flags.shape[2] // devices
    early, late = taps, frames - taps

    halo = shifted(voltages[:, (frames - taps + 1) * length :], "chan", 1)

    order = jnp.arange(devices, dtype=jnp.int32) ^ me
    table = jnp.take(jnp.asarray(dft_table(length)).astype(BF16).reshape(devices, -1, length), order, axis=0)
    late_table = table.reshape(length, length)
    early_table = table.reshape(devices, SPLITS, -1, length).transpose(1, 0, 2, 3).reshape(length, length)

    sent_late = spectra(voltages, None, pfb_taps, late_table, early, late, devices)
    sent_early = spectra(voltages, halo, pfb_taps, early_table, 0, early, devices * SPLITS)

    flags, _ = lax.optimization_barrier((flags, sent_late[0]))
    keep = jnp.repeat(jnp.transpose(flags, (1, 2, 0)).astype(F32), POLS, axis=2)
    keep = jnp.take(keep.reshape(chans, devices, blocks, signals), order, axis=1)
    early_blocks = early * blocks // frames

    def exchanged(block):
        if stns == 2:
            return swapped(block, "stn", 1)
        return lax.all_gather(block, "stn", axis=3, tiled=True)

    def moved(sent, keep, count, begin):
        local, others = [], []
        for g in range(0, devices, GROUP):
            got = [swapped(sent[r], "chan", r) if r else sent[r] for r in range(g, g + GROUP)]
            held = keep[:, g : g + GROUP].reshape(keep.shape[0], -1, signals)
            block = joined(got, held, count)
            local.append((block, begin))
            others.append((exchanged(block), begin))
        return local, others

    local_late, others_late = moved(sent_late, keep[:, :, early_blocks:], late, 0)
    if stns == 2:
        place = lax.axis_index("stn") ^ jnp.arange(2, dtype=jnp.int32)
    else:
        place = jnp.zeros((2,), jnp.int32)
    place = place * (signals // LANES)
    result = None
    part = chans // SPLITS
    for k in range(SPLITS):
        begin = k * part
        local, others = moved(
            sent_early[k * devices : (k + 1) * devices], keep[begin : begin + part, :, :early_blocks], early, begin
        )
        result = correlated(
            result, begin, part, local_late + local, others_late + others, place,
            (chans, 2, signals, signals * stns), 1.0 / total,
        )
    return result


def solution(mesh):
    placed = (P("stn", "chan"), P(), P("stn", "chan", None))
    return jax.shard_map(
        shards, mesh=mesh, in_specs=placed, out_specs=P("chan", None, "stn", None), check_vma=False
    )
```

```python
import functools
import math

import jax
import jax.numpy as jnp
import numpy as np
from jax import lax
from jax.experimental import pallas as pl
from jax.experimental.pallas import tpu as pltpu
from jax.sharding import PartitionSpec as P

POLS = 2
LANES = 128
ROWS = 16
STEP = 8
VMEM = 56 * 1024 * 1024
BF16 = jnp.bfloat16
F32 = jnp.float32


def shifted(block, axis, distance):
    devices = range(lax.axis_size(axis))
    route = [(i - distance, i) for i in devices if i - distance in devices]
    return lax.ppermute(block, axis, route)


def swapped(block, axis, mask):
    return lax.ppermute(block, axis, [(i, i ^ mask) for i in range(lax.axis_size(axis))])


def dft_table(length):
    rows_index = np.arange(length)
    phase = (rows_index // 2)[:, None] * np.arange(length)[None, :] % length
    angles = phase.astype(np.float32) * np.float32(2.0 * math.pi / length)
    values = np.where((rows_index % 2 == 0)[:, None], np.cos(angles), -np.sin(angles))
    return (values / np.float32(math.sqrt(length))).astype(np.float32)


def spectra_kernel(start, count, halos, *refs):
    halo_refs, refs = refs[:halos], refs[halos:]
    volts_ref, taps_ref, table_ref = refs[:3]
    outs, (filt_ref, res_ref) = refs[3:-2], refs[-2:]
    taps, length = taps_ref.shape
    signals = volts_ref.shape[0]

    def frame(rows, j, n0):
        if j < 0:
            piece, at = divmod(j + taps - 1, (taps - 1) // halos)
            return halo_refs[piece][rows, pl.ds(at * length + n0, LANES)].astype(F32)
        return volts_ref[rows, pl.ds(j * length + n0, LANES)].astype(F32)

    def body(g, carry):
        rows = pl.ds(pl.multiple_of(g * ROWS, ROWS), ROWS)
        for n0 in range(0, length, LANES):
            coef = [taps_ref[k : k + 1, n0 : n0 + LANES] for k in range(taps)]
            for t0 in range(0, count, STEP):
                sums = [None] * STEP
                for j in range(start + t0 - (taps - 1), start + t0 + STEP):
                    value = frame(rows, j, n0)
                    for t in range(STEP):
                        k = start + t0 + t - j
                        if 0 <= k < taps:
                            term = coef[k] * value
                            sums[t] = term if sums[t] is None else sums[t] + term
                for t in range(STEP):
                    filt_ref[t0 + t, rows, n0 : n0 + LANES] = sums[t].astype(BF16)
        return carry

    lax.fori_loop(0, signals // ROWS, body, 0)
    for t in range(count):
        res_ref[pl.ds(t, length, stride=count), :] = lax.dot_general(
            table_ref[...], filt_ref[t], (((1,), (1,)), ((), ())), preferred_element_type=F32
        )
    at = 0
    for out in outs:
        out[...] = res_ref[at : at + out.shape[0], :].astype(BF16)
        at += out.shape[0]


def spectra(volts, halos, taps, table, start, count, rows, begin, signals):
    length = taps.shape[1]
    block = min(LANES, signals)
    width = (start + count) * length
    in_specs = [
        pl.BlockSpec((block, width), lambda s: (s + begin // block, 0)),
        pl.BlockSpec(taps.shape, lambda s: (0, 0)),
        pl.BlockSpec(table.shape, lambda s: (0, 0)),
    ]
    args = [*halos, volts, taps, table]
    in_specs = [pl.BlockSpec((block, halo.shape[1]), lambda s: (s, 0)) for halo in halos] + in_specs
    return pl.pallas_call(
        functools.partial(spectra_kernel, start, count, len(halos)),
        grid=(signals // block,),
        in_specs=in_specs,
        out_specs=[pl.BlockSpec((n * count, block), lambda s: (0, s)) for n in rows],
        out_shape=[jax.ShapeDtypeStruct((n * count, signals), BF16) for n in rows],
        scratch_shapes=[
            pltpu.VMEM((count, block, length), BF16),
            pltpu.VMEM((length * count, block), F32),
        ],
        compiler_params=pltpu.CompilerParams(vmem_limit_bytes=VMEM),
        cost_estimate=pl.CostEstimate(
            flops=2 * length * length * count * signals * 5,
            bytes_accessed=2 * signals * (width + length * count),
            transcendentals=0,
        ),
    )(*args)


def join_kernel(count, pieces, *refs):
    held, outs = refs[:pieces], refs[pieces:]
    chans = outs[0].shape[0]
    for m, out in enumerate(outs):
        for c in range(chans):
            values = [
                piece[((m * chans + c) * 2) * count : ((m * chans + c) * 2 + 2) * count, :].astype(F32)
                for piece in held
            ]
            for r in range(2):
                part = [value[r * count : (r + 1) * count] for value in values]
                out[c, r] = jnp.concatenate(part, axis=0).astype(BF16)


def joined(held, outputs, count):
    pieces = len(held)
    rows, signals = held[0].shape
    chans = rows // (outputs * 2 * count)
    block = min(LANES, signals)
    shape = (chans, 2, pieces * count)
    return pl.pallas_call(
        functools.partial(join_kernel, count, pieces),
        grid=(signals // block,),
        in_specs=[pl.BlockSpec((rows, block), lambda s: (0, s))] * pieces,
        out_specs=[pl.BlockSpec(shape + (block,), lambda s: (0, 0, 0, s))] * outputs,
        out_shape=[jax.ShapeDtypeStruct(shape + (signals,), BF16)] * outputs,
        compiler_params=pltpu.CompilerParams(vmem_limit_bytes=VMEM),
        cost_estimate=pl.CostEstimate(
            flops=pieces * rows * signals, bytes_accessed=4 * pieces * rows * signals, transcendentals=0
        ),
    )(*held)


class Block:
    def __init__(self, array, start, count, sources, column, channel):
        self.array, self.start, self.count, self.sources = array, start, count, sources
        self.column, self.channel = column, channel


def correlate_kernel(layout, scale, place_ref, *refs):
    (out_ref, token_ref), (lhs_re, lhs_im, rhs) = refs[-5:-3], refs[-3:]
    token_ref[...] = jnp.zeros_like(token_ref)
    total = rhs.shape[0] // 2
    sides, width, frames = layout["sides"], layout["width"], layout["frames"]
    blocks = layout["blocks"]
    keeps = refs[: sides]
    refs = refs[sides:]
    per = STEP
    for c in range(out_ref.shape[0]):
        for side in range(sides):
            for i, (at, start, count, sources, column, columns) in enumerate(blocks):
                ref = refs[side * len(blocks) + i]
                for r in range(2):
                    values = ref[c, r].astype(F32)
                    rows = []
                    for s, source in enumerate(sources):
                        first = (place_ref[2] ^ source) * (frames // per) + start // per
                        for b in range(count // per):
                            keep = keeps[side][c, pl.ds(first + b, 1), column : column + columns]
                            top = s * count + b * per
                            rows.append(values[top : top + per] * keep)
                    height = count * len(sources)
                    rhs[r * total + at : r * total + at + height, column : column + columns] = jnp.concatenate(
                        rows, axis=0
                    ).astype(BF16)
            if side == 0:
                turned = rhs[...].T
                lhs_re[...] = turned
                lhs_im[:, :total] = turned[:, total:]
                lhs_im[:, total:] = -turned[:, :total]
            columns = pl.ds(pl.multiple_of(place_ref[side] * LANES, LANES), width)
            for r, lhs in enumerate((lhs_re, lhs_im)):
                out_ref[c, r, :, columns] = scale * jnp.dot(lhs[...], rhs[...], preferred_element_type=F32)


def correlated(result, first, chans, local, others, keeps, place, shape, scale, frames, devices):
    step = math.gcd(chans, math.gcd(first, 2))
    signals = shape[2]
    layout = {"sides": len(keeps), "width": signals, "frames": frames, "blocks": []}
    tops, total = {}, 0
    for block in local:
        if block.start not in tops:
            tops[block.start], total = total, total + block.count * devices
        layout["blocks"].append(
            (tops[block.start] + block.sources[0] * block.count, block.start, block.count, block.sources,
             block.column, block.array.shape[3])
        )

    def spec(array, begin):
        return pl.BlockSpec(
            (step,) + array.shape[1:],
            lambda c, place: (c + (first - begin) // step,) + (0,) * (array.ndim - 1),
        )

    in_specs = [spec(keep, 0) for keep in keeps]
    in_specs += [spec(block.array, block.channel) for block in local + others]
    args = list(keeps) + [block.array for block in local + others]
    aliases = {}
    if result is not None:
        in_specs.append(pl.BlockSpec(memory_space=pl.ANY))
        aliases = {1 + len(args): 0}
        args.append(result)
    return pl.pallas_call(
        functools.partial(correlate_kernel, layout, scale),
        grid_spec=pltpu.PrefetchScalarGridSpec(
            num_scalar_prefetch=1,
            grid=(chans // step,),
            in_specs=in_specs,
            out_specs=[
                pl.BlockSpec((step,) + shape[1:], lambda c, place: (c + first // step, 0, 0, 0)),
                pl.BlockSpec((STEP, LANES), lambda c, place: (0, 0)),
            ],
            scratch_shapes=[
                pltpu.VMEM((signals, 2 * total), BF16),
                pltpu.VMEM((signals, 2 * total), BF16),
                pltpu.VMEM((2 * total, signals), BF16),
            ],
        ),
        out_shape=[jax.ShapeDtypeStruct(shape, F32), jax.ShapeDtypeStruct((STEP, LANES), F32)],
        input_output_aliases=aliases,
        compiler_params=pltpu.CompilerParams(vmem_limit_bytes=VMEM),
        cost_estimate=pl.CostEstimate(
            flops=8 * chans * total * signals * shape[3],
            bytes_accessed=4 * chans * 2 * signals * shape[3],
            transcendentals=0,
        ),
    )(place, *args)


def gated(arrays, *tokens):
    n = len(arrays)
    anywhere = pl.BlockSpec(memory_space=pl.ANY)
    return pl.pallas_call(
        lambda *refs: None,
        in_specs=[anywhere] * (n + len(tokens)),
        out_specs=[anywhere] * n,
        out_shape=[jax.ShapeDtypeStruct(array.shape, array.dtype) for array in arrays],
        input_output_aliases={i: i for i in range(n)},
    )(*arrays, *tokens)


class Chunk:
    def __init__(self, near, start, count, column, channel, chans):
        self.near, self.start, self.count, self.column = near, start, count, column
        self.channel, self.chans = channel, chans


def wide_shards(voltages, pfb_taps, flags):
    taps, length = pfb_taps.shape
    signals = voltages.shape[0]
    frames = voltages.shape[1] // length
    devices = lax.axis_size("chan")
    me = lax.axis_index("chan")
    stns = lax.axis_size("stn")
    chans = length // 2 // devices
    total = frames * devices
    early, late = taps, frames - taps
    width = signals // 2

    def halo(half, piece, pieces):
        size = (taps - 1) // pieces * length
        at = (frames - taps + 1) * length + piece * size
        return voltages[half * width : (half + 1) * width, at : at + size]

    halos = [[shifted(halo(0, 0, 1), "chan", 1)], []]

    spread = jnp.repeat(jnp.eye(signals // POLS, dtype=BF16), POLS, axis=1)

    def kept(block):
        return lax.dot_general(block.astype(BF16), spread, (((0,), (0,)), ((), ())), preferred_element_type=F32)

    other_flags = swapped(flags, "stn", 1)
    keeps = [kept(block) for block in (flags, other_flags)]

    table = jnp.asarray(dft_table(length)).astype(BF16).reshape(devices, chans, 2, length)

    def tables(chunks):
        rows = []
        for chunk in chunks:
            order = np.arange(devices).reshape(-1, chunk.near).T.reshape(-1)
            part = jnp.take(table[:, chunk.channel : chunk.channel + chunk.chans], me ^ order, axis=0)
            rows.append(part.reshape(-1, length))
        sizes = [part.shape[0] // chunk.near for part, chunk in zip(rows, chunks) for _ in range(chunk.near)]
        return jnp.concatenate(rows, axis=0), sizes

    chunks = [Chunk(NEARS[0], early, late, 0, 0, chans), Chunk(NEARS[1], 0, early, 0, 0, chans)]
    begin = 0
    for part, close in zip(SPLITS, NEARS[2:]):
        size = chans * part // sum(SPLITS)
        chunks.append(Chunk(close, 0, early, width, begin, size))
        begin += size
    kernels = [(chunks[:1], None, 0, signals), (chunks[1:2], 0, 0, width), (chunks[2:], 1, width, width)]

    sent, ready, arrived, crossed = {}, {}, {}, {}
    def ordered(orders):
        counts = [devices // chunk.near for chunk in chunks]
        return [(k, m) for k, n in enumerate(counts) for m in orders.get(n, range(n))]

    units, issued = ordered(SWAPS), ordered(SENDS)
    first = {}
    for i, (k, m) in enumerate(units):
        first.setdefault(k, i)

    def compute(n, token):
        group, half, column, size = kernels[n]
        rows, sizes = tables(group)
        before = [] if half is None else halos[half]
        if before:
            before = gated(before, token)
        outs = spectra(voltages, before, pfb_taps, rows, group[0].start, group[0].count, sizes, column, size)
        outs = list(outs)
        for chunk in group:
            sent[chunks.index(chunk)] = outs[: chunk.near]
            outs = outs[chunk.near :]

    def near(k):
        sent[k] = [swapped(piece, "chan", s) if s else piece for s, piece in enumerate(sent[k])]

    def join(k):
        for m, block in enumerate(joined(sent[k], devices // chunks[k].near, chunks[k].count)):
            ready[k, m] = block

    def far(k, m):
        arrived[k, m] = swapped(ready[k, m], "chan", m * chunks[k].near) if m else ready[k, m]

    place = (lax.axis_index("stn") ^ jnp.arange(stns, dtype=jnp.int32)) * (signals // LANES)
    place = jnp.concatenate([place, me[None].astype(jnp.int32)])

    def correlate(k, result):
        last = chunks[k]
        local, others = [], []
        for n, m in units:
            chunk = chunks[n]
            if n < 2 or n == k:
                for side, have in ((local, arrived), (others, crossed)):
                    sources = range(m * chunk.near, (m + 1) * chunk.near)
                    side.append(Block(have[n, m], chunk.start, chunk.count, sources, chunk.column, chunk.channel))
        return correlated(
            result, last.channel, last.chans, local, others, keeps, place,
            (chans, 2, signals, signals * stns), 1.0 / total, frames, devices,
        )

    result, marks = None, {}
    compute(0, None)
    near(0)
    join(0)
    token = sent[0][0]
    for u in issued[:AHEAD]:
        far(*u)
    pieces = PIECES if (taps - 1) % PIECES == 0 else 1
    for i in range(len(units)):
        for n, (group, half, _, _) in enumerate(kernels):
            if n and max(first[chunks.index(group[0])] - AHEAD - LEAD, 0) == i:
                compute(n, token)
        passed = [(arrived, units[i])]
        nears = [k for k in first if k and first[k] - AHEAD - 2 == i]
        joins = [k for k in first if k and first[k] - AHEAD - 1 == i]
        fars = issued[i + AHEAD : i + AHEAD + 1]
        for k in nears + joins:
            passed += [(sent[k], s) for s in range(len(sent[k]))]
        for u in fars:
            passed.append((ready, u))
        tokens = [token]
        if i >= DEPTH:
            tokens.append(crossed[units[i - DEPTH]])
        if i == 1:
            tokens.append(other_flags)
        for mark in marks.pop(i, []):
            tokens.append(mark)
        outs = list(gated([where[key] for where, key in passed], *tokens))
        for (where, key), out in zip(passed, outs):
            where[key] = out
        token = outs[0]
        for k in nears:
            near(k)
        for k in joins:
            join(k)
        crossed[units[i]] = swapped(arrived[units[i]], "stn", 1)
        for u in fars:
            far(*u)
        if 0 <= FIRST_PIECE <= i < FIRST_PIECE + pieces:
            piece = gated([halo(1, i - FIRST_PIECE, pieces)], token)[0]
            halos[1].append(shifted(piece, "chan", 1))
            marks.setdefault(i + 2, []).append(halos[1][-1])
        for k in first:
            if k >= 2 and k + 1 in first and i == first[k + 1] + LATER:
                result, mark = correlate(k, result)
                marks.setdefault(i + 1, []).append(mark)
    return correlate(len(chunks) - 1, result)[0]


SWAPS = {8: (0, 2, 4, 3, 6, 1, 5, 7), 4: (0, 2, 1, 3)}
SENDS = {8: (0, 2, 4, 3, 6, 1, 5, 7), 4: (0, 2, 1, 3)}
AHEAD = 3
DEPTH = 2
LEAD = 3
NEARS = (2, 4, 4, 4)
SPLITS = (1, 1)
FIRST_PIECE = 4
PIECES = 1
LATER = 3


def cross_tile(local, remote, count):
    prods = jnp.einsum("cpat,cqbt->cpqab", local, remote, preferred_element_type=jnp.float32)
    real_part = prods[:, 0, 0] + prods[:, 1, 1]
    imag_part = prods[:, 1, 0] - prods[:, 0, 1]
    return jnp.stack([real_part, imag_part], axis=1) / count


def narrow_shards(voltages, pfb_taps, flags):
    taps, length = pfb_taps.shape
    signals = voltages.shape[0]
    frames_here = voltages.shape[1] // length
    frames = voltages.reshape(signals, frames_here, length)
    earlier = shifted(frames[:, frames_here - (taps - 1) :, :], "chan", 1)
    padded = jnp.concatenate([earlier, frames], axis=1)
    filtered = jnp.zeros((signals, frames_here, length), F32)
    for k in range(taps):
        offset = taps - 1 - k
        filtered = filtered + pfb_taps[k] * padded[:, offset : offset + frames_here, :]
    filtered = filtered.astype(BF16)
    table = jnp.asarray(dft_table(length)).astype(BF16)
    spectra = jnp.einsum("qn,stn->qst", table, filtered, preferred_element_type=F32).astype(BF16)
    turned = lax.all_to_all(spectra, "chan", split_axis=0, concat_axis=2, tiled=True)
    chans, total = turned.shape[0] // 2, turned.shape[2]
    stations, _, blocks = flags.shape
    keep = jnp.transpose(flags, (1, 0, 2)).astype(BF16)[:, None, :, None, :, None]
    shaped = turned.reshape(chans, 2, stations, POLS, blocks, total // blocks)
    weighted = (shaped * keep).reshape(chans, 2, signals, total)
    return cross_tile(weighted, lax.all_gather(weighted, "stn", axis=2, tiled=True), float(total))


def shards(voltages, pfb_taps, flags):
    if lax.axis_size("stn") != 2 or voltages.shape[0] % (2 * LANES) or lax.axis_size("chan") % NEARS[-1]:
        return narrow_shards(voltages, pfb_taps, flags)
    return wide_shards(voltages, pfb_taps, flags)


def solution(mesh):
    placed = (P("stn", "chan"), P(), P("stn", "chan", None))
    return jax.shard_map(
        shards, mesh=mesh, in_specs=placed, out_specs=P("chan", None, "stn", None), check_vma=False
    )
```

```python
import functools
import math

import jax
import jax.numpy as jnp
import numpy as np
from jax import lax
from jax.experimental import pallas as pl
from jax.experimental.pallas import tpu as pltpu
from jax.sharding import PartitionSpec as P

POLS = 2
LANES = 128
ROWS = 16
STEP = 8
VMEM = 56 * 1024 * 1024
BF16 = jnp.bfloat16
F32 = jnp.float32


def shifted(block, axis, distance):
    devices = range(lax.axis_size(axis))
    route = [(i - distance, i) for i in devices if i - distance in devices]
    return lax.ppermute(block, axis, route)


def swapped(block, axis, mask):
    return lax.ppermute(block, axis, [(i, i ^ mask) for i in range(lax.axis_size(axis))])


def dft_table(length):
    rows_index = np.arange(length)
    phase = (rows_index // 2)[:, None] * np.arange(length)[None, :] % length
    angles = phase.astype(np.float32) * np.float32(2.0 * math.pi / length)
    values = np.where((rows_index % 2 == 0)[:, None], np.cos(angles), -np.sin(angles))
    return (values / np.float32(math.sqrt(length))).astype(np.float32)


def spectra_kernel(start, count, halos, *refs):
    halo_refs, refs = refs[:halos], refs[halos:]
    volts_ref, taps_ref, table_ref = refs[:3]
    outs, (filt_ref, res_ref) = refs[3:-2], refs[-2:]
    taps, length = taps_ref.shape
    signals = volts_ref.shape[0]

    def frame(rows, j, n0):
        if j < 0:
            piece, at = divmod(j + taps - 1, (taps - 1) // halos)
            return halo_refs[piece][rows, pl.ds(at * length + n0, LANES)].astype(F32)
        return volts_ref[rows, pl.ds(j * length + n0, LANES)].astype(F32)

    def body(g, carry):
        rows = pl.ds(pl.multiple_of(g * ROWS, ROWS), ROWS)
        for n0 in range(0, length, LANES):
            coef = [taps_ref[k : k + 1, n0 : n0 + LANES] for k in range(taps)]
            for t0 in range(0, count, STEP):
                sums = [None] * STEP
                for j in range(start + t0 - (taps - 1), start + t0 + STEP):
                    value = frame(rows, j, n0)
                    for t in range(STEP):
                        k = start + t0 + t - j
                        if 0 <= k < taps:
                            term = coef[k] * value
                            sums[t] = term if sums[t] is None else sums[t] + term
                for t in range(STEP):
                    filt_ref[t0 + t, rows, n0 : n0 + LANES] = sums[t].astype(BF16)
        return carry

    lax.fori_loop(0, signals // ROWS, body, 0)
    for t in range(count):
        res_ref[pl.ds(t, length, stride=count), :] = lax.dot_general(
            table_ref[...], filt_ref[t], (((1,), (1,)), ((), ())), preferred_element_type=F32
        )
    at = 0
    for out in outs:
        out[...] = res_ref[at : at + out.shape[0], :].astype(BF16)
        at += out.shape[0]


def spectra(volts, halos, taps, table, start, count, rows, begin, signals):
    length = taps.shape[1]
    block = min(LANES, signals)
    width = (start + count) * length
    in_specs = [
        pl.BlockSpec((block, width), lambda s: (s + begin // block, 0)),
        pl.BlockSpec(taps.shape, lambda s: (0, 0)),
        pl.BlockSpec(table.shape, lambda s: (0, 0)),
    ]
    args = [*halos, volts, taps, table]
    in_specs = [pl.BlockSpec((block, halo.shape[1]), lambda s: (s, 0)) for halo in halos] + in_specs
    return pl.pallas_call(
        functools.partial(spectra_kernel, start, count, len(halos)),
        grid=(signals // block,),
        in_specs=in_specs,
        out_specs=[pl.BlockSpec((n * count, block), lambda s: (0, s)) for n in rows],
        out_shape=[jax.ShapeDtypeStruct((n * count, signals), BF16) for n in rows],
        scratch_shapes=[
            pltpu.VMEM((count, block, length), BF16),
            pltpu.VMEM((length * count, block), F32),
        ],
        compiler_params=pltpu.CompilerParams(vmem_limit_bytes=VMEM),
        cost_estimate=pl.CostEstimate(
            flops=2 * length * length * count * signals * 5,
            bytes_accessed=2 * signals * (width + length * count),
            transcendentals=0,
        ),
    )(*args)


def join_kernel(count, pieces, *refs):
    held, outs = refs[:pieces], refs[pieces:]
    chans = outs[0].shape[0]
    for m, out in enumerate(outs):
        for c in range(chans):
            values = [
                piece[((m * chans + c) * 2) * count : ((m * chans + c) * 2 + 2) * count, :].astype(F32)
                for piece in held
            ]
            for r in range(2):
                part = [value[r * count : (r + 1) * count] for value in values]
                out[c, r] = jnp.concatenate(part, axis=0).astype(BF16)


def joined(held, outputs, count):
    pieces = len(held)
    rows, signals = held[0].shape
    chans = rows // (outputs * 2 * count)
    block = min(LANES, signals)
    shape = (chans, 2, pieces * count)
    return pl.pallas_call(
        functools.partial(join_kernel, count, pieces),
        grid=(signals // block,),
        in_specs=[pl.BlockSpec((rows, block), lambda s: (0, s))] * pieces,
        out_specs=[pl.BlockSpec(shape + (block,), lambda s: (0, 0, 0, s))] * outputs,
        out_shape=[jax.ShapeDtypeStruct(shape + (signals,), BF16)] * outputs,
        compiler_params=pltpu.CompilerParams(vmem_limit_bytes=VMEM),
        cost_estimate=pl.CostEstimate(
            flops=pieces * rows * signals, bytes_accessed=4 * pieces * rows * signals, transcendentals=0
        ),
    )(*held)


class Block:
    def __init__(self, array, start, count, sources, column, channel):
        self.array, self.start, self.count, self.sources = array, start, count, sources
        self.column, self.channel = column, channel


def correlate_kernel(layout, scale, place_ref, *refs):
    (out_ref, token_ref), (lhs, rhs) = refs[-4:-2], refs[-2:]
    token_ref[...] = jnp.zeros_like(token_ref)
    total = rhs.shape[0] // 2
    sides, width, frames = layout["sides"], layout["width"], layout["frames"]
    blocks = layout["blocks"]
    keeps = refs[: sides]
    refs = refs[sides:]
    per = STEP
    for c in range(out_ref.shape[0]):
        for side in range(sides):
            for i, (at, start, count, sources, column, columns) in enumerate(blocks):
                ref = refs[side * len(blocks) + i]
                for r in range(2):
                    values = ref[c, r].astype(F32)
                    rows = []
                    for s, source in enumerate(sources):
                        first = (place_ref[2] ^ source) * (frames // per) + start // per
                        for b in range(count // per):
                            keep = keeps[side][c, pl.ds(first + b, 1), column : column + columns]
                            top = s * count + b * per
                            rows.append(values[top : top + per] * keep)
                    height = count * len(sources)
                    rhs[r * total + at : r * total + at + height, column : column + columns] = jnp.concatenate(
                        rows, axis=0
                    ).astype(BF16)
            if side == 0:
                turned = rhs[...].T
                lhs[:width, :] = turned
                lhs[width:, :total] = turned[:, total:]
                lhs[width:, total:] = -turned[:, :total]
            columns = pl.ds(pl.multiple_of(place_ref[side] * LANES, LANES), width)
            both = scale * jnp.dot(lhs[...], rhs[...], preferred_element_type=F32)
            for r in range(2):
                out_ref[c, r, :, columns] = both[r * width : (r + 1) * width]


def correlated(result, first, chans, local, others, keeps, place, shape, scale, frames, devices):
    step = math.gcd(chans, math.gcd(first, 2))
    signals = shape[2]
    layout = {"sides": len(keeps), "width": signals, "frames": frames, "blocks": []}
    tops, total = {}, 0
    for block in local:
        if block.start not in tops:
            tops[block.start], total = total, total + block.count * devices
        layout["blocks"].append(
            (tops[block.start] + block.sources[0] * block.count, block.start, block.count, block.sources,
             block.column, block.array.shape[3])
        )

    def spec(array, begin):
        return pl.BlockSpec(
            (step,) + array.shape[1:],
            lambda c, place: (c + (first - begin) // step,) + (0,) * (array.ndim - 1),
        )

    in_specs = [spec(keep, 0) for keep in keeps]
    in_specs += [spec(block.array, block.channel) for block in local + others]
    args = list(keeps) + [block.array for block in local + others]
    aliases = {}
    if result is not None:
        in_specs.append(pl.BlockSpec(memory_space=pl.ANY))
        aliases = {1 + len(args): 0}
        args.append(result)
    return pl.pallas_call(
        functools.partial(correlate_kernel, layout, scale),
        grid_spec=pltpu.PrefetchScalarGridSpec(
            num_scalar_prefetch=1,
            grid=(chans // step,),
            in_specs=in_specs,
            out_specs=[
                pl.BlockSpec((step,) + shape[1:], lambda c, place: (c + first // step, 0, 0, 0)),
                pl.BlockSpec((STEP, LANES), lambda c, place: (0, 0)),
            ],
            scratch_shapes=[
                pltpu.VMEM((2 * signals, 2 * total), BF16),
                pltpu.VMEM((2 * total, signals), BF16),
            ],
        ),
        out_shape=[jax.ShapeDtypeStruct(shape, F32), jax.ShapeDtypeStruct((STEP, LANES), F32)],
        input_output_aliases=aliases,
        compiler_params=pltpu.CompilerParams(vmem_limit_bytes=VMEM),
        cost_estimate=pl.CostEstimate(
            flops=8 * chans * total * signals * shape[3],
            bytes_accessed=4 * chans * 2 * signals * shape[3],
            transcendentals=0,
        ),
    )(place, *args)


def gated(arrays, *tokens):
    n = len(arrays)
    anywhere = pl.BlockSpec(memory_space=pl.ANY)
    return pl.pallas_call(
        lambda *refs: None,
        in_specs=[anywhere] * (n + len(tokens)),
        out_specs=[anywhere] * n,
        out_shape=[jax.ShapeDtypeStruct(array.shape, array.dtype) for array in arrays],
        input_output_aliases={i: i for i in range(n)},
    )(*arrays, *tokens)


class Chunk:
    def __init__(self, near, start, count, column, channel, chans):
        self.near, self.start, self.count, self.column = near, start, count, column
        self.channel, self.chans = channel, chans


def wide_shards(voltages, pfb_taps, flags):
    taps, length = pfb_taps.shape
    signals = voltages.shape[0]
    frames = voltages.shape[1] // length
    devices = lax.axis_size("chan")
    me = lax.axis_index("chan")
    stns = lax.axis_size("stn")
    chans = length // 2 // devices
    total = frames * devices
    early, late = taps, frames - taps
    width = signals // 2

    def halo(half, piece, pieces):
        size = (taps - 1) // pieces * length
        at = (frames - taps + 1) * length + piece * size
        return voltages[half * width : (half + 1) * width, at : at + size]

    halos = [[shifted(halo(0, 0, 1), "chan", 1)], []]

    spread = jnp.repeat(jnp.eye(signals // POLS, dtype=BF16), POLS, axis=1)

    def kept(block):
        return lax.dot_general(block.astype(BF16), spread, (((0,), (0,)), ((), ())), preferred_element_type=F32)

    other_flags = swapped(flags, "stn", 1)
    keeps = [kept(block) for block in (flags, other_flags)]

    table = jnp.asarray(dft_table(length)).astype(BF16).reshape(devices, chans, 2, length)

    def tables(chunks):
        rows = []
        for chunk in chunks:
            order = np.arange(devices).reshape(-1, chunk.near).T.reshape(-1)
            part = jnp.take(table[:, chunk.channel : chunk.channel + chunk.chans], me ^ order, axis=0)
            rows.append(part.reshape(-1, length))
        sizes = [part.shape[0] // chunk.near for part, chunk in zip(rows, chunks) for _ in range(chunk.near)]
        return jnp.concatenate(rows, axis=0), sizes

    chunks = [Chunk(NEARS[0], early, late, 0, 0, chans), Chunk(NEARS[1], 0, early, 0, 0, chans)]
    begin = 0
    for part, close in zip(SPLITS, NEARS[2:]):
        size = chans * part // sum(SPLITS)
        chunks.append(Chunk(close, 0, early, width, begin, size))
        begin += size
    kernels = [(chunks[:1], None, 0, signals), (chunks[1:2], 0, 0, width), (chunks[2:], 1, width, width)]

    sent, ready, arrived, crossed = {}, {}, {}, {}
    def ordered(orders):
        counts = [devices // chunk.near for chunk in chunks]
        return [(k, m) for k, n in enumerate(counts) for m in orders.get(n, range(n))]

    units, issued = ordered(SWAPS), ordered(SENDS)
    first = {}
    for i, (k, m) in enumerate(units):
        first.setdefault(k, i)

    def compute(n, token):
        group, half, column, size = kernels[n]
        rows, sizes = tables(group)
        before = [] if half is None else halos[half]
        if before:
            before = gated(before, token)
        outs = spectra(voltages, before, pfb_taps, rows, group[0].start, group[0].count, sizes, column, size)
        outs = list(outs)
        for chunk in group:
            sent[chunks.index(chunk)] = outs[: chunk.near]
            outs = outs[chunk.near :]

    def near(k):
        sent[k] = [swapped(piece, "chan", s) if s else piece for s, piece in enumerate(sent[k])]

    def join(k):
        for m, block in enumerate(joined(sent[k], devices // chunks[k].near, chunks[k].count)):
            ready[k, m] = block

    def far(k, m):
        arrived[k, m] = swapped(ready[k, m], "chan", m * chunks[k].near) if m else ready[k, m]

    place = (lax.axis_index("stn") ^ jnp.arange(stns, dtype=jnp.int32)) * (signals // LANES)
    place = jnp.concatenate([place, me[None].astype(jnp.int32)])

    def correlate(k, result):
        last = chunks[k]
        local, others = [], []
        for n, m in units:
            chunk = chunks[n]
            if n < 2 or n == k:
                for side, have in ((local, arrived), (others, crossed)):
                    sources = range(m * chunk.near, (m + 1) * chunk.near)
                    side.append(Block(have[n, m], chunk.start, chunk.count, sources, chunk.column, chunk.channel))
        return correlated(
            result, last.channel, last.chans, local, others, keeps, place,
            (chans, 2, signals, signals * stns), 1.0 / total, frames, devices,
        )

    result, marks = None, {}
    compute(0, None)
    near(0)
    join(0)
    token = sent[0][0]
    for u in issued[:AHEAD]:
        far(*u)
    pieces = PIECES if (taps - 1) % PIECES == 0 else 1
    for i in range(len(units)):
        for n, (group, half, _, _) in enumerate(kernels):
            if n and max(first[chunks.index(group[0])] - AHEAD - LEAD, 0) == i:
                compute(n, token)
        passed = [(arrived, units[i])]
        nears = [k for k in first if k and first[k] - AHEAD - 2 == i]
        joins = [k for k in first if k and first[k] - AHEAD - 1 == i]
        fars = issued[i + AHEAD : i + AHEAD + 1]
        for k in nears + joins:
            passed += [(sent[k], s) for s in range(len(sent[k]))]
        for u in fars:
            passed.append((ready, u))
        tokens = [token]
        if i >= DEPTH:
            tokens.append(crossed[units[i - DEPTH]])
        if i == 1:
            tokens.append(other_flags)
        for mark in marks.pop(i, []):
            tokens.append(mark)
        outs = list(gated([where[key] for where, key in passed], *tokens))
        for (where, key), out in zip(passed, outs):
            where[key] = out
        token = outs[0]
        for k in nears:
            near(k)
        for k in joins:
            join(k)
        crossed[units[i]] = swapped(arrived[units[i]], "stn", 1)
        for u in fars:
            far(*u)
        if 0 <= FIRST_PIECE <= i < FIRST_PIECE + pieces:
            piece = gated([halo(1, i - FIRST_PIECE, pieces)], token)[0]
            halos[1].append(shifted(piece, "chan", 1))
            marks.setdefault(i + 2, []).append(halos[1][-1])
        for k in first:
            if k >= 2 and k + 1 in first and i == first[k + 1] + LATER:
                result, mark = correlate(k, result)
                marks.setdefault(i + 1, []).append(mark)
    return correlate(len(chunks) - 1, result)[0]


SWAPS = {8: (0, 2, 4, 3, 6, 1, 5, 7), 4: (0, 2, 1, 3)}
SENDS = {8: (0, 2, 4, 3, 6, 1, 5, 7), 4: (0, 2, 1, 3)}
AHEAD = 3
DEPTH = 2
LEAD = 4
NEARS = (2, 4, 4, 4)
SPLITS = (1, 1)
FIRST_PIECE = 3
PIECES = 1
LATER = 3


def cross_tile(local, remote, count):
    prods = jnp.einsum("cpat,cqbt->cpqab", local, remote, preferred_element_type=jnp.float32)
    real_part = prods[:, 0, 0] + prods[:, 1, 1]
    imag_part = prods[:, 1, 0] - prods[:, 0, 1]
    return jnp.stack([real_part, imag_part], axis=1) / count


def narrow_shards(voltages, pfb_taps, flags):
    taps, length = pfb_taps.shape
    signals = voltages.shape[0]
    frames_here = voltages.shape[1] // length
    frames = voltages.reshape(signals, frames_here, length)
    earlier = shifted(frames[:, frames_here - (taps - 1) :, :], "chan", 1)
    padded = jnp.concatenate([earlier, frames], axis=1)
    filtered = jnp.zeros((signals, frames_here, length), F32)
    for k in range(taps):
        offset = taps - 1 - k
        filtered = filtered + pfb_taps[k] * padded[:, offset : offset + frames_here, :]
    filtered = filtered.astype(BF16)
    table = jnp.asarray(dft_table(length)).astype(BF16)
    spectra = jnp.einsum("qn,stn->qst", table, filtered, preferred_element_type=F32).astype(BF16)
    turned = lax.all_to_all(spectra, "chan", split_axis=0, concat_axis=2, tiled=True)
    chans, total = turned.shape[0] // 2, turned.shape[2]
    stations, _, blocks = flags.shape
    keep = jnp.transpose(flags, (1, 0, 2)).astype(BF16)[:, None, :, None, :, None]
    shaped = turned.reshape(chans, 2, stations, POLS, blocks, total // blocks)
    weighted = (shaped * keep).reshape(chans, 2, signals, total)
    return cross_tile(weighted, lax.all_gather(weighted, "stn", axis=2, tiled=True), float(total))


def shards(voltages, pfb_taps, flags):
    if lax.axis_size("stn") != 2 or voltages.shape[0] % (2 * LANES) or lax.axis_size("chan") % NEARS[-1]:
        return narrow_shards(voltages, pfb_taps, flags)
    return wide_shards(voltages, pfb_taps, flags)


def solution(mesh):
    placed = (P("stn", "chan"), P(), P("stn", "chan", None))
    return jax.shard_map(
        shards, mesh=mesh, in_specs=placed, out_specs=P("chan", None, "stn", None), check_vma=False
    )
```
